32 devices in a mesh: row: 4 (over y, core), col: 8 (over z, x).
Axes of the slice: x: 2, y: 2, z: 4, core: 2. Of those that a mesh axis runs over, the one named last changes fastest.
Arguments:
- stored: float32 [16384, 16384], P('row', 'col'), may hold values from -1 to 2.5, as said below
Outputs:
- factored: float32 [16384, 16384], P('row', 'col')
The draws below stay inside these ranges and needn't reach their ends.
Inputs may be any that keep to these rules, and one draw needn't show every extreme that they name: `stored`: symmetric positive definite with smallest eigenvalue at least 0.25: a Rotne-Prager-Yamakawa mobility of beads of unit radius (3 x 3 blocks per pair, correlation-regularized, self-mobility scaled to 1; the last rows beyond a multiple of 3 are unit diagonal) with perturbed off-diagonal entries, plus a positive diagonal.
All inputs are finite; a program needn't handle non-finite values.
Results may differ from the reference program's by a relative error of at most 0.0001.
Values sent between devices are 32-bit elements; how exact they have to be, the bound alone decides.
No kernel may reach another device: no remote copies, remote signals or barrier semaphores. Data moves between devices by JAX's collectives and lax.ppermute only.
A program may use at most 192 MiB of HBM per device.

```python
import jax
import jax.numpy as jnp
from jax import lax

TRAIL = 16384
NB = 256
PANELS = 2
N_ROW = 4
N_COL = 8


def draw_stored(key, part):
    order = TRAIL
    beads = order // 3
    used = 3 * beads
    side = (beads * 4.18879 / 0.1) ** (1.0 / 3.0)
    coords = jax.random.uniform(jax.random.fold_in(key, 11), (3, beads), jnp.float32)
    coords = coords * side
    nugget = jax.random.uniform(jax.random.fold_in(key, 12), (order,), jnp.float32, 0.5, 1.5)
    deltas = [coords[axis][:, None] - coords[axis][None, :] for axis in range(3)]
    square = deltas[0] * deltas[0] + deltas[1] * deltas[1] + deltas[2] * deltas[2]
    dist = jnp.sqrt(jnp.maximum(square, 1e-12))
    inverse = 1.0 / dist
    far_iso = 0.75 * inverse * (1.0 + 2.0 / 3.0 * inverse * inverse)
    far_pair = 0.75 * inverse * (1.0 - 2.0 * inverse * inverse) * inverse * inverse
    near_iso = 1.0 - 9.0 * dist / 32.0
    near_pair = 3.0 / 32.0 * inverse
    apart = dist >= 2.0
    selfmask = jnp.eye(beads, dtype=jnp.bool_)
    iso = jnp.where(selfmask, 1.0, jnp.where(apart, far_iso, near_iso))
    pair = jnp.where(selfmask, 0.0, jnp.where(apart, far_pair, near_pair))
    blocks = []
    for first in range(3):
        line = []
        for second in range(3):
            entry = pair * deltas[first] * deltas[second]
            if first == second:
                entry = entry + iso
            line.append(entry)
        blocks.append(jnp.stack(line, 0))
    mobility = jnp.stack(blocks, 0).transpose(2, 0, 3, 1).reshape(used, used)
    index = jnp.arange(order, dtype=jnp.int32)
    natural = jnp.zeros((order, order), jnp.float32).at[:used, :used].set(mobility)
    jitter = jax.random.uniform(jax.random.fold_in(key, 13), (order, order), jnp.float32, -1.0, 1.0)
    offdiag = index[:, None] != index[None, :]
    natural = natural + jnp.where(offdiag, 0.001 * (jitter + jitter.T), 0.0)
    natural = natural + jnp.diag(nugget + jnp.where(index >= used, 1.0, 0.0))
    rt = order // (NB * N_ROW)
    ct = order // (NB * N_COL)
    return natural.reshape(rt, N_ROW, NB, ct, N_COL, NB).transpose(1, 0, 2, 4, 3, 5).reshape(order, order).astype(jnp.float32)


def setup_inputs(seed: int = 0) -> dict:
    arg_keys = jax.random.split(jax.random.key(seed), 2)
    return {
        "stored": draw_stored(jax.random.fold_in(arg_keys[1], 71), 0),
    }


def to_natural(stored):
    order = stored.shape[0]
    rt = order // (NB * N_ROW)
    ct = order // (NB * N_COL)
    return stored.reshape(N_ROW, rt, NB, N_COL, ct, NB).transpose(1, 0, 2, 4, 3, 5).reshape(order, order)

def to_stored(natural):
    order = natural.shape[0]
    rt = order // (NB * N_ROW)
    ct = order // (NB * N_COL)
    return natural.reshape(rt, N_ROW, NB, ct, N_COL, NB).transpose(1, 0, 2, 4, 3, 5).reshape(order, order)

def reference(stored):
    matrix = to_natural(stored)
    for k in range(PANELS):
        start = k * NB
        stop = start + NB
        lower = jnp.linalg.cholesky(matrix[start:stop, start:stop])
        below = jax.scipy.linalg.solve_triangular(lower, matrix[stop:, start:stop].T, lower=True).T
        matrix = matrix.at[start:stop, start:stop].set(lower)
        matrix = matrix.at[stop:, start:stop].set(below)
        matrix = matrix.at[:start, start:stop].set(jnp.float32(0.0))
        update = jnp.dot(below.astype(jnp.float32), below.T.astype(jnp.float32), precision=lax.Precision.HIGHEST, preferred_element_type=jnp.float32)
        matrix = matrix.at[stop:, stop:].add(-update)
    matrix = matrix.at[:PANELS * NB, PANELS * NB:].set(jnp.float32(0.0))
    return to_stored(matrix)
```

```python
import functools

import jax
import jax.numpy as jnp
import numpy as np
from jax import lax
from jax.experimental import pallas as pl
from jax.experimental.pallas import tpu as pltpu
from jax.sharding import PartitionSpec as P

NB = 256
PANELS = 2
WIDE = PANELS * NB
STEP = 128
SUB = 8
HIGHEST = lax.Precision.HIGHEST
F32 = jnp.float32
BF16 = jnp.bfloat16


def col_coords(mesh):
    cols = mesh.shape["col"]
    try:
        return [tuple(int(c) for c in d.coords) for d in np.asarray(mesh.devices)[0]]
    except AttributeError:
        return [(q // 2, q % 2) for q in range(cols)]


def col_ports(coords):
    where = {c: i for i, c in enumerate(coords)}
    ports = []
    for d in range(len(coords[0])):
        size = max(c[d] for c in coords) - min(c[d] for c in coords) + 1
        found = []
        for step in (1, -1):
            pairs = []
            for i, c in enumerate(coords):
                t = c[:d] + (c[d] + step,) + c[d + 1 :]
                if t in where:
                    pairs.append((i, where[t]))
            if pairs:
                found.append(pairs)
        if size == 2:
            ports.append(found[0] + found[1])
        else:
            ports.extend(found)
    return ports


def spread(nodes, ports, homes, avail, tries):
    items = len(homes)
    edges = [(i, j, k) for k, pairs in enumerate(ports) for i, j in pairs]
    best = None
    for attempt in range(tries):
        rng = np.random.RandomState(attempt)
        ready = np.full((nodes, items), 10**6)
        for it, home in enumerate(homes):
            ready[home, it] = avail[it]
        got = ready < 10**6
        slots = []
        while not got.all() and len(slots) < 500 and (best is None or len(slots) < len(best)):
            slot = len(slots)
            moves = []
            count = got.sum(0).astype(float)
            new = got.copy()
            rem = list(range(len(edges)))
            while rem:
                can = [(ready[edges[e][0]] <= slot) & ~new[edges[e][1]] for e in rem]
                rem = [e for e, o in zip(rem, can) if o.any()]
                can = [o for o in can if o.any()]
                if not rem:
                    break
                x = min(range(len(rem)), key=lambda x: can[x].sum() + rng.rand() * 2)
                i, j, k = edges[rem[x]]
                it = min(np.flatnonzero(can[x]), key=lambda it: count[it] + rng.rand() * 0.5)
                moves.append((k, i, j, int(it)))
                new[j, it] = True
                count[it] += 1
                rem.pop(x)
            for k, i, j, it in moves:
                ready[j, it] = slot + 1
            got = new
            slots.append(moves)
        if got.all() and (best is None or len(slots) < len(best)):
            best = slots
    return best


def make_plan(mesh, rtiles, ctiles):
    rows, cols = mesh.shape["row"], mesh.shape["col"]
    groups = min(4, ctiles)
    per = ctiles // groups
    ports = col_ports(col_coords(mesh))
    tries = 60 if cols <= 8 else 2
    plans = []
    for p in range(rows):
        homes = [(p + rows * i) % cols for i in range(rtiles)]
        layer = p // PANELS
        avail = [
            0 if layer == 0 else layer + ((p + rows * i) // cols) // per for i in range(rtiles)
        ]
        plans.append(spread(cols, ports, homes, avail, tries))
    nslots = max(len(s) for s in plans)
    sends = []
    for t in range(nslots):
        row = []
        for k in range(len(ports)):
            perm = []
            for p in range(rows):
                if t < len(plans[p]):
                    perm += [(p * cols + i, p * cols + j) for kk, i, j, _ in plans[p][t] if kk == k]
            if perm:
                row.append((k, tuple(perm)))
        sends.append(row)
    buf = {}
    for t in range(nslots):
        for k, _ in sends[t]:
            buf[(t, k)] = len(buf) + 1
    held = {}
    pack = [np.full((rows * cols, max(1, len(sends[t])), 2), -1, np.int32) for t in range(nslots)]
    for p in range(rows):
        for i in range(rtiles):
            held[(p, (p + rows * i) % cols, i)] = (0, -1)
        for t, moves in enumerate(plans[p]):
            index = {k: n for n, (k, _) in enumerate(sends[t])}
            for k, a, b, it in moves:
                source = held[(p, a, it)][0]
                pack[t][p * cols + a, index[k]] = (source, (p + rows * it) // cols)
                held[(p, b, it)] = (buf[(t, k)], t)
    order = np.zeros((rows * cols, rtiles, 4), np.int32)
    when = np.zeros((rows * cols, rtiles), np.int32)
    for p in range(rows):
        for q in range(cols):
            mine = sorted(range(rtiles), key=lambda i: (held[(p, q, i)][1], i))
            for n, i in enumerate(mine):
                source, slot = held[(p, q, i)]
                order[p * cols + q, n] = (i, p + rows * i, source, (p + rows * i) // cols)
                when[p * cols + q, n] = slot
    return groups, sends, buf, pack, order, when


def any_spec():
    return pl.BlockSpec(memory_space=pl.ANY)


def pack_kernel(groups, per, sources, nout, tab, *refs):
    stored, other = refs[0], refs[1]
    own_g = refs[2 : 2 + groups]
    oth_g = refs[2 + groups : 2 + 2 * groups]
    recv = refs[2 + 2 * groups : 2 + 2 * groups + len(sources)]
    outs = refs[2 + 2 * groups + len(sources) : -1]
    sem = refs[-1]
    lane, layer = tab[2 * nout], tab[2 * nout + 1]

    def each(act):
        for n in range(nout):
            source, j = tab[2 * n], tab[2 * n + 1]
            out = outs[n]
            for k in range(PANELS):
                rows = pl.ds(k * NB, NB)

                def go(src, half, k=k, n=n, out=out, rows=rows):
                    act(pltpu.make_async_copy(src, out.at[rows, :], sem.at[n]))

                cols = pl.ds(pl.multiple_of(jnp.maximum(j, 0) * NB, NB), NB)

                @pl.when((source == 0) & (layer == 0) & (lane == k))
                def _():
                    go(stored.at[pl.ds(0, NB), cols], k)

                @pl.when((source == 0) & (layer == 0) & (lane != k))
                def _():
                    go(other.at[:, cols], k)

                for g in range(groups):
                    near = pl.ds(pl.multiple_of((jnp.maximum(j, 0) % per) * NB, NB), NB)

                    @pl.when((source == 0) & (layer > 0) & (j // per == g) & (lane == k))
                    def _(g=g, near=near):
                        go(own_g[g].at[:, near], k)

                    @pl.when((source == 0) & (layer > 0) & (j // per == g) & (lane != k))
                    def _(g=g, near=near):
                        go(oth_g[g].at[:, near], k)

            for r, b in enumerate(sources):

                @pl.when(source == b)
                def _(r=r, n=n, out=out):
                    act(pltpu.make_async_copy(recv[r], out, sem.at[n]))

    each(lambda c: c.start())
    each(lambda c: c.wait())


def pack(tab, stored, other, own_g, oth_g, sources, recv, nout):
    groups = len(own_g)
    per = stored.shape[1] // NB // groups
    args = [stored, other, *own_g, *oth_g, *recv]
    return pl.pallas_call(
        functools.partial(pack_kernel, groups, per, sources, nout),
        grid_spec=pltpu.PrefetchScalarGridSpec(
            num_scalar_prefetch=1,
            grid=(),
            in_specs=[any_spec()] * len(args),
            out_specs=[any_spec()] * nout,
            scratch_shapes=[pltpu.SemaphoreType.DMA((nout,))],
        ),
        out_shape=[jax.ShapeDtypeStruct((WIDE, NB), F32)] * nout,
        cost_estimate=pl.CostEstimate(
            flops=0, bytes_accessed=8 * nout * WIDE * NB, transcendentals=0
        ),
        name="pack",
    )(tab, *args)


def dot(a, b, dims):
    return lax.dot_general(
        a, b, ((dims[0], dims[1]), ((), ())), precision=HIGHEST, preferred_element_type=F32
    )


def eliminate(work, start):
    rows = work[start : start + SUB, :]
    lanes = rows.shape[1]
    sub = lax.broadcasted_iota(jnp.int32, (SUB, STEP), 0)
    cols = [
        jnp.broadcast_to(rows[:, start + c : start + c + 1], (SUB, STEP)) for c in range(SUB)
    ]
    parts = [rows[:, a : a + STEP] for a in range(0, lanes, STEP)]
    for c in range(SUB):
        pivot = jnp.broadcast_to(cols[c][c : c + 1, :], (SUB, STEP))
        root = lax.rsqrt(pivot)
        root = root * (1.5 - 0.5 * pivot * root * root)
        factor = jnp.where(sub > c, cols[c] * root, 0.0)
        scale = jnp.where(sub == c, root, 1.0)

        def step(x, c=c, root=root, factor=factor, scale=scale):
            line = jnp.broadcast_to(x[c : c + 1, :], (SUB, STEP)) * root
            return x * scale - factor * line

        parts = [step(x) for x in parts]
        for d in range(c + 1, SUB):
            cols[d] = step(cols[d])
    return jnp.concatenate(parts, 1)


def factor_kernel(block, s_ref, u_in, v_in, u_ref, v_ref, work):
    lo, hi = block * STEP, (block + 1) * STEP
    u_ref[...] = u_in[...]
    v_ref[...] = v_in[...]
    row = s_ref[lo:hi, :]
    eye = (
        lax.broadcasted_iota(jnp.int32, (STEP, STEP), 0)
        == lax.broadcasted_iota(jnp.int32, (STEP, STEP), 1)
    ).astype(F32)
    if lo:
        left = u_in[0:lo, lo:hi]
        row = row - dot(left, u_in[0:lo, :], ((0,), (0,)))
        inv = -dot(left, v_in[0:lo, 0:lo], ((0,), (0,)))
    work[:, 0:STEP] = row[:, lo:hi]
    work[:, STEP:] = eye
    lanes = lax.broadcasted_iota(jnp.int32, (SUB, 2 * STEP), 1)
    for start in range(0, STEP, SUB):
        done = eliminate(work, start)
        work[start : start + SUB, :] = jnp.where(lanes >= start, done, 0.0)
        if start + SUB < STEP:
            rest = work[start + SUB :, :]
            work[start + SUB :, :] = rest - dot(
                done[:, start + SUB : STEP], done, ((0,), (0,))
            )
    dinv = work[:, STEP:]
    u_ref[lo:hi, lo:hi] = work[:, 0:STEP]
    v_ref[lo:hi, lo:hi] = dinv
    if hi < WIDE:
        u_ref[lo:hi, hi:] = dot(dinv, row[:, hi:], ((1,), (0,)))
    if lo:
        v_ref[lo:hi, 0:lo] = dot(dinv, inv, ((1,), (0,)))


def factor(block, s, u, v):
    return pl.pallas_call(
        functools.partial(factor_kernel, block),
        out_shape=[jax.ShapeDtypeStruct((WIDE, WIDE), F32)] * 2,
        scratch_shapes=[pltpu.VMEM((STEP, 2 * STEP), F32)],
        input_output_aliases={1: 0, 2: 1},
        compiler_params=pltpu.CompilerParams(vmem_limit_bytes=32 * 2**20),
        cost_estimate=pl.CostEstimate(
            flops=6 * 10**9, bytes_accessed=6 * 2**20, transcendentals=0
        ),
        name="factor",
    )(s, u, v)


def split(x):
    high = x.astype(BF16)
    return high, (x - high.astype(F32)).astype(BF16)


def right_kernel(tab, v_ref, b_ref, hi_ref, lo_ref, sinv):
    @pl.when(pl.program_id(0) == 0)
    def _():
        sinv[...] = dot(v_ref[...], v_ref[...], ((0,), (0,)))

    r = dot(sinv[...], b_ref[...], ((1,), (0,)))
    high, low = split(r)
    hi_ref[...] = high
    lo_ref[...] = low
    for k in range(PANELS):

        @pl.when((pl.program_id(0) == 0) & (tab[0] == k))
        def _(k=k):
            high, low = split(-v_ref[k * NB : (k + 1) * NB, :].T)
            hi_ref[:, 0:NB] = high
            lo_ref[:, 0:NB] = low


def right(tab, v, b):
    cols = b.shape[1]
    wide = min(cols, 512)
    return pl.pallas_call(
        right_kernel,
        grid_spec=pltpu.PrefetchScalarGridSpec(
            num_scalar_prefetch=1,
            grid=(cols // wide,),
            in_specs=[
                pl.BlockSpec((WIDE, WIDE), lambda c, t: (0, 0)),
                pl.BlockSpec((WIDE, wide), lambda c, t: (0, c)),
            ],
            out_specs=[pl.BlockSpec((WIDE, wide), lambda c, t: (0, c))] * 2,
            scratch_shapes=[pltpu.VMEM((WIDE, WIDE), F32)],
        ),
        out_shape=[jax.ShapeDtypeStruct((WIDE, cols), BF16)] * 2,
        compiler_params=pltpu.CompilerParams(vmem_limit_bytes=32 * 2**20),
        cost_estimate=pl.CostEstimate(
            flops=12 * WIDE * WIDE * cols, bytes_accessed=10 * WIDE * cols, transcendentals=0
        ),
        name="right",
    )(tab, v, b)


def update_kernel(count, sources, head, tab, m_ref, hi_ref, lo_ref, b_ref, *refs):
    recv = refs[: len(sources)]
    out_ref, lhs, sem = refs[-3], refs[-2], refs[-1]
    s = pl.program_id(0)
    mine = tab[4 * count]

    def fetch(n, act):
        source, j = tab[4 * n + 2], tab[4 * n + 3]
        slot = lax.rem(n, 2)
        cols = pl.ds(pl.multiple_of(j * NB, NB), NB)

        @pl.when(source == 0)
        def _():
            act(pltpu.make_async_copy(b_ref.at[:, cols], lhs.at[slot], sem.at[slot]))

        for r, b in enumerate(sources):

            @pl.when(source == b)
            def _(r=r):
                act(pltpu.make_async_copy(recv[r], lhs.at[slot], sem.at[slot]))

    @pl.when(s == 0)
    def _():
        fetch(s, lambda c: c.start())

    @pl.when(s + 1 < count)
    def _():
        fetch(s + 1, lambda c: c.start())

    fetch(s, lambda c: c.wait())
    high, low = split(lhs[lax.rem(s, 2)].T)
    cols = m_ref.shape[1]

    def mm(a, b):
        return jnp.dot(a, b, preferred_element_type=F32)

    for a in range(0, cols, NB):
        rh, rl = hi_ref[:, a : a + NB], lo_ref[:, a : a + NB]
        prod = mm(high, rh) + (mm(high, rl) + mm(low, rh))
        m = m_ref[:, a : a + NB]
        if a == 0:
            m = jnp.where(mine < PANELS, 0.0, m)
        out_ref[:, a : a + NB] = m - prod
    tile = tab[4 * s + 1]

    @pl.when(tile < PANELS)
    def _():
        r = lax.broadcasted_iota(jnp.int32, (NB, NB), 0)
        c = lax.broadcasted_iota(jnp.int32, (NB, NB), 1)
        keep = (mine < PANELS) & ((tile > mine) | ((tile == mine) & (r >= c)))
        out_ref[:, 0:NB] = jnp.where(keep, out_ref[:, 0:NB], 0.0)
        if cols > NB:
            out_ref[:, NB:] = jnp.zeros((NB, cols - NB), F32)


def update(tab, count, stored, high, low, b, sources, recv, prev):
    nrows, cols = stored.shape
    args = [stored, high, low, b, *recv] + ([] if prev is None else [prev])
    whole = pl.BlockSpec((WIDE, cols), lambda s, t: (0, 0), pipeline_mode=pl.Buffered(1))
    return pl.pallas_call(
        functools.partial(update_kernel, count, sources, prev is None),
        grid_spec=pltpu.PrefetchScalarGridSpec(
            num_scalar_prefetch=1,
            grid=(count,),
            in_specs=[pl.BlockSpec((NB, cols), lambda s, t: (t[4 * s], 0)), whole, whole]
            + [any_spec()] * (len(args) - 3),
            out_specs=pl.BlockSpec((NB, cols), lambda s, t: (t[4 * s], 0)),
            scratch_shapes=[pltpu.VMEM((2, WIDE, NB), F32), pltpu.SemaphoreType.DMA((2,))],
        ),
        out_shape=jax.ShapeDtypeStruct((nrows, cols), F32),
        input_output_aliases={} if prev is None else {len(args): 0},
        compiler_params=pltpu.CompilerParams(vmem_limit_bytes=40 * 2**20),
        cost_estimate=pl.CostEstimate(
            flops=6 * count * NB * WIDE * cols,
            bytes_accessed=8 * count * NB * cols + 4 * WIDE * cols,
            transcendentals=0,
        ),
        name="update",
    )(tab, *args)


def local(plan, mesh, stored):
    groups, sends, buf, packs, order, when = plan
    rows, cols = mesh.shape["row"], mesh.shape["col"]
    layers = rows // PANELS
    both = ("row", "col")
    my_row, my_col = lax.axis_index("row"), lax.axis_index("col")
    me = my_row * cols + my_col
    lane, layer = my_row % PANELS, my_row // PANELS
    ctiles = stored.shape[1] // NB
    gcols = ctiles // groups * NB

    def at(p, q):
        return p * cols + q

    first = stored[0:NB, 0:NB]
    s = jnp.concatenate(
        [
            jnp.concatenate(
                [
                    jnp.where((my_row == k) & (my_col == j), first, F32(0.0))
                    for j in range(PANELS)
                ],
                1,
            )
            for k in range(PANELS)
        ],
        0,
    )
    s = lax.psum(s, both)

    top = stored[0:NB, :]
    swap = [
        (at(p, q), at(p ^ 1, q)) for p in range(PANELS) for q in range(cols)
    ]
    other = lax.ppermute(top, both, swap)
    own_g, oth_g = [], []
    for g in range(groups):
        cur = stored[0:NB, g * gcols : (g + 1) * gcols]
        own = cur
        for l in range(1, layers):
            perm = [
                (at((l - 1) * PANELS + c, q), at(l * PANELS + c, q))
                for c in range(PANELS)
                for q in range(cols)
            ]
            cur = lax.ppermute(cur, both, perm)
            own = cur if layers == 2 else jnp.where(layer == l, cur, own)
        own_g.append(own)
        perm = [
            (at(p, q), at(p ^ 1, q)) for p in range(PANELS, rows) for q in range(cols)
        ]
        oth_g.append(lax.ppermute(own, both, perm))

    recv = {}
    for t, ops in enumerate(sends):
        live = sorted(
            {int(b) for b in np.unique(packs[t][:, :, 0]) if b > 0}
        )
        nout = len(ops)
        tab = jnp.concatenate(
            [
                jnp.asarray(packs[t].reshape(rows * cols, -1))[me],
                jnp.stack([lane, layer]).astype(jnp.int32),
            ]
        )
        use = min(groups, max(1, t))
        og = [own_g[min(g, use - 1)] for g in range(groups)]
        hg = [oth_g[min(g, use - 1)] for g in range(groups)]
        outs = pack(tab, stored, other, og, hg, live, [recv[b] for b in live], nout)
        for (k, perm), out in zip(ops, outs):
            recv[buf[(t, k)]] = lax.ppermute(out, both, perm)

    u = jnp.zeros((WIDE, WIDE), F32)
    v = jnp.zeros((WIDE, WIDE), F32)
    for block in range(WIDE // STEP):
        u, v = factor(block, s, u, v)

    halves = []
    for k in range(PANELS):
        near = jnp.where(lane == k, top, other)
        far = jnp.where(
            lane == k, jnp.concatenate(own_g, 1), jnp.concatenate(oth_g, 1)
        )
        halves.append(jnp.where(layer == 0, near, far))
    b = jnp.concatenate(halves, 0)
    flag = my_col.astype(jnp.int32)[None]
    high, low = right(flag, v, b)

    rtiles = stored.shape[0] // NB
    nslots = len(sends)
    cuts = [int((when <= nslots - 4).sum(1).min()), int((when <= nslots - 2).sum(1).min()), rtiles]
    table = jnp.asarray(order)[me]
    out = None
    start = 0
    for stop in cuts:
        if stop <= start:
            continue
        count = stop - start
        live = sorted({int(x) for x in np.unique(order[:, start:stop, 2]) if x > 0})
        tab = jnp.concatenate([table[start:stop].reshape(-1), flag])
        out = update(tab, count, stored, high, low, b, live, [recv[x] for x in live], out)
        start = stop
    return out


def solution(mesh):
    placed = (P("row", "col"),)

    def whole(stored):
        rtiles = stored.shape[0] // mesh.shape["row"] // NB
        ctiles = stored.shape[1] // mesh.shape["col"] // NB
        plan = make_plan(mesh, rtiles, ctiles)
        return jax.shard_map(
            functools.partial(local, plan, mesh),
            mesh=mesh,
            in_specs=placed,
            out_specs=P("row", "col"),
            check_vma=False,
        )(stored)

    return whole
```

```python
import functools

import jax
import jax.numpy as jnp
from jax import lax
from jax.experimental import pallas as pl
from jax.experimental.pallas import tpu as pltpu
from jax.sharding import PartitionSpec as P

NB = 256
PANELS = 2
WIDE = PANELS * NB
STEP = 128
SUB = 8
ROOM = 58 * 2**20
HIGHEST = lax.Precision.HIGHEST
F32 = jnp.float32
BF16 = jnp.bfloat16


def any_spec():
    return pl.BlockSpec(memory_space=pl.ANY)


def dot(a, b, dims):
    return lax.dot_general(
        a, b, ((dims[0], dims[1]), ((), ())), precision=HIGHEST, preferred_element_type=F32
    )


def eliminate(work, start):
    rows = work[start : start + SUB, :]
    lanes = rows.shape[1]
    sub = lax.broadcasted_iota(jnp.int32, (SUB, STEP), 0)
    cols = [
        jnp.broadcast_to(rows[:, start + c : start + c + 1], (SUB, STEP)) for c in range(SUB)
    ]
    parts = [rows[:, a : a + STEP] for a in range(0, lanes, STEP)]
    for c in range(SUB):
        pivot = jnp.broadcast_to(cols[c][c : c + 1, :], (SUB, STEP))
        root = lax.rsqrt(pivot)
        root = root * (1.5 - 0.5 * pivot * root * root)
        factor = jnp.where(sub > c, cols[c] * root, 0.0)
        scale = jnp.where(sub == c, root, 1.0)

        def step(x, c=c, root=root, factor=factor, scale=scale):
            line = jnp.broadcast_to(x[c : c + 1, :], (SUB, STEP)) * root
            return x * scale - factor * line

        parts = [step(x) for x in parts]
        for d in range(c + 1, SUB):
            cols[d] = step(cols[d])
    return jnp.concatenate(parts, 1)


def factor_kernel(block, s_ref, u_in, v_in, u_ref, v_ref, work):
    lo, hi = block * STEP, (block + 1) * STEP
    u_ref[...] = u_in[...]
    v_ref[...] = v_in[...]
    row = s_ref[lo:hi, :]
    eye = (
        lax.broadcasted_iota(jnp.int32, (STEP, STEP), 0)
        == lax.broadcasted_iota(jnp.int32, (STEP, STEP), 1)
    ).astype(F32)
    if lo:
        left = u_in[0:lo, lo:hi]
        row = row - dot(left, u_in[0:lo, :], ((0,), (0,)))
        inv = -dot(left, v_in[0:lo, 0:lo], ((0,), (0,)))
    work[:, 0:STEP] = row[:, lo:hi]
    work[:, STEP:] = eye
    lanes = lax.broadcasted_iota(jnp.int32, (SUB, 2 * STEP), 1)
    for start in range(0, STEP, SUB):
        done = eliminate(work, start)
        work[start : start + SUB, :] = jnp.where(lanes >= start, done, 0.0)
        if start + SUB < STEP:
            rest = work[start + SUB :, :]
            work[start + SUB :, :] = rest - dot(
                done[:, start + SUB : STEP], done, ((0,), (0,))
            )
    dinv = work[:, STEP:]
    u_ref[lo:hi, lo:hi] = work[:, 0:STEP]
    v_ref[lo:hi, lo:hi] = dinv
    if hi < WIDE:
        u_ref[lo:hi, hi:] = dot(dinv, row[:, hi:], ((1,), (0,)))
    if lo:
        v_ref[lo:hi, 0:lo] = dot(dinv, inv, ((1,), (0,)))


def factor(block, s, u, v):
    return pl.pallas_call(
        functools.partial(factor_kernel, block),
        out_shape=[jax.ShapeDtypeStruct((WIDE, WIDE), F32)] * 2,
        scratch_shapes=[pltpu.VMEM((STEP, 2 * STEP), F32)],
        input_output_aliases={1: 0, 2: 1},
        compiler_params=pltpu.CompilerParams(vmem_limit_bytes=ROOM),
        cost_estimate=pl.CostEstimate(
            flops=6 * 10**9, bytes_accessed=6 * 2**20, transcendentals=0
        ),
        name="factor",
    )(s, u, v)


def split(x):
    high = x.astype(BF16)
    return high, (x - high.astype(F32)).astype(BF16)


def right_kernel(tab, v_ref, b_ref, hi_ref, lo_ref, sinv):
    mine, side = tab[0], tab[1]

    @pl.when(pl.program_id(0) == 0)
    def _():
        sinv[...] = dot(v_ref[...], v_ref[...], ((0,), (0,)))

    def place(k):
        return pl.ds(pl.multiple_of(lax.rem(k + PANELS - side, PANELS) * NB, NB), NB)

    for k in range(PANELS):
        high, low = split(dot(sinv[k * NB : (k + 1) * NB, :], b_ref[...], ((1,), (0,))))
        hi_ref[place(k), :] = high
        lo_ref[place(k), :] = low
    for j in range(PANELS):

        @pl.when((pl.program_id(0) == 0) & (mine == j))
        def _(j=j):
            for k in range(PANELS):
                high, low = split(-v_ref[j * NB : (j + 1) * NB, k * NB : (k + 1) * NB].T)
                hi_ref[place(k), 0:NB] = high
                lo_ref[place(k), 0:NB] = low


def right(tab, v, b):
    cols = b.shape[1]
    wide = min(cols, 512)
    return pl.pallas_call(
        right_kernel,
        grid_spec=pltpu.PrefetchScalarGridSpec(
            num_scalar_prefetch=1,
            grid=(cols // wide,),
            in_specs=[
                pl.BlockSpec((WIDE, WIDE), lambda c, t: (0, 0)),
                pl.BlockSpec((WIDE, wide), lambda c, t: (0, c)),
            ],
            out_specs=[pl.BlockSpec((WIDE, wide), lambda c, t: (0, c))] * 2,
            scratch_shapes=[pltpu.VMEM((WIDE, WIDE), F32)],
        ),
        out_shape=[jax.ShapeDtypeStruct((WIDE, cols), BF16)] * 2,
        compiler_params=pltpu.CompilerParams(vmem_limit_bytes=ROOM),
        cost_estimate=pl.CostEstimate(
            flops=12 * WIDE * WIDE * cols, bytes_accessed=10 * WIDE * cols, transcendentals=0
        ),
        name="right",
    )(tab, v, b)


def update_kernel(first, count, nbuf, tab, m_ref, hi_ref, lo_ref, *refs):
    own, other = refs[:nbuf], refs[nbuf : 2 * nbuf]
    out_ref, lhs, sem = refs[-3], refs[-2], refs[-1]
    s = pl.program_id(0)
    chain, mine, my_row = tab[0], tab[1], tab[2]

    def fetch(n, act):
        slot = lax.rem(n, 2)
        for x in range(nbuf):

            @pl.when(n + chain == x)
            def _(x=x):
                act(pltpu.make_async_copy(own[x], lhs.at[slot, 0], sem.at[slot, 0]))
                act(pltpu.make_async_copy(other[x], lhs.at[slot, 1], sem.at[slot, 1]))

    @pl.when(s == 0)
    def _():
        fetch(s, lambda c: c.start())

    @pl.when(s + 1 < count)
    def _():
        fetch(s + 1, lambda c: c.start())

    fetch(s, lambda c: c.wait())
    slot = lax.rem(s, 2)
    oh, ol = split(lhs[slot, 0])
    th, tl = split(lhs[slot, 1])
    left = jnp.concatenate([oh, th, oh, th, ol, tl], 1)
    cols = m_ref.shape[1]
    for a in range(0, cols, NB):
        rh, rl = hi_ref[:, a : a + NB], lo_ref[:, a : a + NB]
        prod = jnp.dot(
            left, jnp.concatenate([rh, rl, rh], 0), preferred_element_type=F32
        )
        m = m_ref[:, a : a + NB]
        if a == 0:
            m = jnp.where(mine < PANELS, 0.0, m)
        out_ref[:, a : a + NB] = m - prod
    if first == 0:

        @pl.when((s == 0) & (my_row < PANELS))
        def _():
            r = lax.broadcasted_iota(jnp.int32, (NB, NB), 0)
            c = lax.broadcasted_iota(jnp.int32, (NB, NB), 1)
            keep = (mine < PANELS) & ((my_row > mine) | ((my_row == mine) & (r >= c)))
            out_ref[0:NB, 0:NB] = jnp.where(keep, out_ref[0:NB, 0:NB], 0.0)
            if cols > NB:
                out_ref[0:NB, NB:] = jnp.zeros((NB, cols - NB), F32)


def update(tab, first, count, stored, high, low, own, other, prev):
    nrows, cols = stored.shape
    tall = own[0].shape[0]
    args = [stored, high, low, *own, *other] + ([] if prev is None else [prev])
    whole = pl.BlockSpec((WIDE, cols), lambda s, t: (0, 0), pipeline_mode=pl.Buffered(1))
    return pl.pallas_call(
        functools.partial(update_kernel, first, count, len(own)),
        grid_spec=pltpu.PrefetchScalarGridSpec(
            num_scalar_prefetch=1,
            grid=(count,),
            in_specs=[pl.BlockSpec((tall, cols), lambda s, t: (first + s, 0)), whole, whole]
            + [any_spec()] * (len(args) - 3),
            out_specs=pl.BlockSpec((tall, cols), lambda s, t: (first + s, 0)),
            scratch_shapes=[
                pltpu.VMEM((2, PANELS, tall, NB), F32),
                pltpu.SemaphoreType.DMA((2, PANELS)),
            ],
        ),
        out_shape=jax.ShapeDtypeStruct((nrows, cols), F32),
        input_output_aliases={} if prev is None else {len(args): 0},
        compiler_params=pltpu.CompilerParams(vmem_limit_bytes=ROOM),
        cost_estimate=pl.CostEstimate(
            flops=6 * count * tall * WIDE * cols,
            bytes_accessed=8 * count * tall * cols + 4 * WIDE * cols,
            transcendentals=0,
        ),
        name="update",
    )(tab, *args)


def after(x, *done):
    return lax.optimization_barrier((x, *done))[0]


def local(mesh, stored):
    rows, cols = mesh.shape["row"], mesh.shape["col"]
    layers, length = rows // PANELS, cols // PANELS
    both = ("row", "col")
    my_row, my_col = lax.axis_index("row"), lax.axis_index("col")
    layer, lane = my_row // PANELS, my_row % PANELS
    link, side = my_col // PANELS, my_col % PANELS
    rtiles = stored.shape[0] // NB
    tall = (2 if rtiles % 2 == 0 else 1) * NB
    pieces = stored.shape[0] // tall
    nsteps = pieces + length - 1
    devices = [
        (y, c, l, f)
        for y in range(layers)
        for c in range(PANELS)
        for l in range(length)
        for f in range(PANELS)
    ]

    def at(y, c, l, f):
        return (y * PANELS + c) * cols + l * PANELS + f

    def move(x, to):
        pairs = [(at(*d), at(*t)) for d in devices if (t := to(*d)) is not None]
        return lax.ppermute(x, both, pairs)

    def pair(flag, x, y, axis):
        return jnp.concatenate([jnp.where(flag, y, x), jnp.where(flag, x, y)], axis)

    corner = stored[0:NB, 0:NB]
    block = corner
    hops = [
        move(corner, lambda y, c, l, f, h=h: (y, c, h, f) if (y, l) == (0, 0) else None)
        for h in range(1, length)
    ]

    def panel(s):
        return stored[s * tall : (s + 1) * tall, 0:NB]

    own, other, along = [], [], None

    def send(s, *done):
        if s == 0:
            cur = panel(0)
        elif s < pieces:
            cur = jnp.where(link == 0, panel(s), along)
        else:
            cur = along
        if done:
            cur = after(cur, *done)
        own.append(cur)
        z = None
        if s < nsteps - 1:
            z = move(
                cur,
                lambda y, c, l, f: (y, c, l + 1, f)
                if 0 <= s - l < pieces and l + 1 < length
                else None,
            )
        other.append(
            move(cur, lambda y, c, l, f: (y, c, l, 1 - f) if 0 <= s - l < pieces else None)
        )
        return z

    along = send(0)
    for h, x in enumerate(hops):
        block = jnp.where(link == h + 1, x, block)
    near, far = block, block
    cross = move(block, lambda y, c, l, f: (y, c, l, 1 - f) if y == 0 else None)
    for h in range(1, layers):
        x = move(block, lambda y, c, l, f: (h, c, l, f) if y == 0 else None)
        y_ = move(block, lambda y, c, l, f: (h, c, l, 1 - f) if y == 0 else None)
        near = jnp.where(layer == h, x, near)
        cross = jnp.where(layer == h, y_, cross)
    line = pair(side == 1, near, cross, 1)
    s_all = pair(lane == 1, line, move(line, lambda y, c, l, f: (y, 1 - c, l, f)), 0)

    along = send(1)
    top = after(stored[0:NB, :], near, cross)
    cur, half = top, top
    for h in range(1, layers):
        cur = move(cur, lambda y, c, l, f: (h, c, l, f) if y == h - 1 else None)
        half = jnp.where(layer == h, cur, half)
    mate = move(half, lambda y, c, l, f: (y, 1 - c, l, f))

    flags = jnp.stack([link, my_col, my_row, side]).astype(jnp.int32)
    u = jnp.zeros((WIDE, WIDE), F32)
    v = jnp.zeros((WIDE, WIDE), F32)
    nblocks = WIDE // STEP
    start = min(3, nsteps - 1)
    out, rest = None, 0
    high = low = None
    todo = [("factor", k) for k in range(nblocks)] + [("right", 0)]
    for s in range(2, nsteps):
        dep = []
        if s > start and todo:
            kind, k = todo.pop(0)
            if kind == "factor":
                u, v = factor(k, after(s_all, own[s - 1]) if k == 0 else s_all, u, v)
                dep = [v]
            else:
                b = pair(lane == 1, half, mate, 0)
                high, low = right(jnp.stack([my_col, side]).astype(jnp.int32), v, b)
                dep = [low]
        elif s > start and high is not None:
            stop = min(rest + 2, s - length + 1, pieces)
            if stop > rest:
                out = run_update(flags, rest, stop, stored, high, low, own, other, out, length)
                rest = stop
                dep = [out]
        along = send(s, *dep, other[s - 2])
    for kind, k in todo:
        if kind == "factor":
            u, v = factor(k, s_all, u, v)
        else:
            b = pair(lane == 1, half, mate, 0)
            high, low = right(jnp.stack([my_col, side]).astype(jnp.int32), v, b)
    cuts = [x for x in (pieces - 2, pieces - 1, pieces) if x > rest]
    for stop in cuts:
        out = run_update(flags, rest, stop, stored, high, low, own, other, out, length)
        rest = stop
    return out


def run_update(flags, first, stop, stored, high, low, own, other, prev, length):
    lo, hi = first, stop + length - 1
    return update(
        flags, first, stop - first, stored, high, low, own[lo:hi], other[lo:hi], prev
    )


def solution(mesh):
    return jax.shard_map(
        functools.partial(local, mesh),
        mesh=mesh,
        in_specs=(P("row", "col"),),
        out_specs=P("row", "col"),
        check_vma=False,
    )
```

```python
import functools

import jax
import jax.numpy as jnp
from jax import lax
from jax.experimental import pallas as pl
from jax.experimental.pallas import tpu as pltpu
from jax.sharding import PartitionSpec as P

NB = 256
PANELS = 2
WIDE = PANELS * NB
STEP = 128
SUB = 16
ROOM = 58 * 2**20
HIGHEST = lax.Precision.HIGHEST
F32 = jnp.float32
BF16 = jnp.bfloat16


def any_spec():
    return pl.BlockSpec(memory_space=pl.ANY)


def dot(a, b, dims):
    return lax.dot_general(
        a, b, ((dims[0], dims[1]), ((), ())), precision=HIGHEST, preferred_element_type=F32
    )


def eliminate(work, start):
    rows = work[start : start + SUB, :]
    lanes = rows.shape[1]
    shape = (SUB, STEP)
    sub = lax.broadcasted_iota(jnp.int32, shape, 0)
    cols = [jnp.broadcast_to(rows[:, start + c : start + c + 1], shape) for c in range(SUB)]
    parts = [rows[:, a : a + STEP] for a in range(0, lanes, STEP)]
    scale = jnp.ones(shape, F32)

    def line(x, c):
        return jnp.broadcast_to(x[c : c + 1, :], shape)

    def inverse(x):
        r = pl.reciprocal(x, approx=True)
        r = r * (2.0 - x * r)
        return r * (2.0 - x * r)

    for c in range(0, SUB, 2):
        p, q = cols[c], cols[c + 1]
        a, b, d = line(p, c), line(q, c), line(q, c + 1)
        det = a * d - b * b
        r, ra = inverse(det), inverse(a)
        f = jnp.where(sub > c + 1, (p * d - q * b) * r, jnp.where(sub == c + 1, b * ra, 0.0))
        g = jnp.where(sub > c + 1, (q * a - p * b) * r, 0.0)
        scale = jnp.where(sub == c, a, jnp.where(sub == c + 1, det * ra, scale))
        for e in range(c + 2, SUB):
            cols[e] = cols[e] - f * line(cols[e], c) - g * line(cols[e], c + 1)
        parts = [x - f * line(x, c) - g * line(x, c + 1) for x in parts]
    root = lax.rsqrt(scale)
    root = root * (1.5 - 0.5 * scale * root * root)
    return jnp.concatenate([x * root for x in parts], 1)


def factor_kernel(block, s_ref, *refs):
    us, vs = refs[:block], refs[block : 2 * block]
    u_ref, v_ref, work = refs[2 * block :]
    lo, hi = block * STEP, (block + 1) * STEP
    eye = (
        lax.broadcasted_iota(jnp.int32, (STEP, STEP), 0)
        == lax.broadcasted_iota(jnp.int32, (STEP, STEP), 1)
    ).astype(F32)
    row = s_ref[:, lo:]
    if lo:
        left = jnp.concatenate([x[:, lo:hi] for x in us], 0)
        row = row - dot(left, jnp.concatenate([x[:, lo:] for x in us], 0), ((0,), (0,)))
        inv = -dot(left, jnp.concatenate([x[:, 0:lo] for x in vs], 0), ((0,), (0,)))
        u_ref[:, 0:lo] = jnp.zeros((STEP, lo), F32)
    work[:, 0:STEP] = row[:, 0:STEP]
    work[:, STEP:] = eye
    lanes = lax.broadcasted_iota(jnp.int32, (SUB, 2 * STEP), 1)
    for start in range(0, STEP, SUB):
        done = eliminate(work, start)
        work[start : start + SUB, :] = jnp.where(lanes >= start, done, 0.0)
        if start + SUB < STEP:
            rest = work[start + SUB :, :]
            work[start + SUB :, :] = rest - dot(
                done[:, start + SUB : STEP], done, ((0,), (0,))
            )
    dinv = work[:, STEP:]
    u_ref[:, lo:hi] = work[:, 0:STEP]
    v_ref[:, lo:hi] = dinv
    if hi < WIDE:
        u_ref[:, hi:] = dot(dinv, row[:, STEP:], ((1,), (0,)))
        v_ref[:, hi:] = jnp.zeros((STEP, WIDE - hi), F32)
    if lo:
        v_ref[:, 0:lo] = dot(dinv, inv, ((1,), (0,)))


def factor(s, us, vs):
    block = len(us)
    line = pl.BlockSpec((STEP, WIDE), lambda i: (0, 0))
    return pl.pallas_call(
        functools.partial(factor_kernel, block),
        grid=(1,),
        in_specs=[pl.BlockSpec((STEP, WIDE), lambda i: (block, 0))] + [line] * (2 * block),
        out_specs=[line] * 2,
        out_shape=[jax.ShapeDtypeStruct((STEP, WIDE), F32)] * 2,
        scratch_shapes=[pltpu.VMEM((STEP, 2 * STEP), F32)],
        compiler_params=pltpu.CompilerParams(vmem_limit_bytes=24 * 2**20),
        cost_estimate=pl.CostEstimate(
            flops=6 * 10**9, bytes_accessed=6 * 2**20, transcendentals=0
        ),
        name="factor",
    )(s, *us, *vs)


def split(x):
    high = x.astype(BF16)
    return high, (x - high.astype(F32)).astype(BF16)


def right_kernel(blocks, tab, *refs):
    vs = refs[:blocks]
    b_ref, hi_ref, lo_ref, sinv = refs[blocks:]
    mine, side = tab[0], tab[1]

    @pl.when(pl.program_id(0) == 0)
    def _():
        v = jnp.concatenate([x[...] for x in vs], 0)
        sinv[...] = dot(v, v, ((0,), (0,)))

    def place(k):
        return pl.ds(pl.multiple_of(lax.rem(k + PANELS - side, PANELS) * NB, NB), NB)

    for k in range(PANELS):
        high, low = split(dot(sinv[k * NB : (k + 1) * NB, :], b_ref[...], ((1,), (0,))))
        hi_ref[place(k), :] = high
        lo_ref[place(k), :] = low
    for j in range(PANELS):

        @pl.when((pl.program_id(0) == 0) & (mine == j))
        def _(j=j):
            for k in range(PANELS):
                for m in range(NB // STEP):
                    part = vs[j * (NB // STEP) + m][:, k * NB : (k + 1) * NB]
                    high, low = split(-part.T)
                    hi_ref[place(k), m * STEP : (m + 1) * STEP] = high
                    lo_ref[place(k), m * STEP : (m + 1) * STEP] = low


def right(tab, vs, b):
    cols = b.shape[1]
    wide = min(cols, 512)
    return pl.pallas_call(
        functools.partial(right_kernel, len(vs)),
        grid_spec=pltpu.PrefetchScalarGridSpec(
            num_scalar_prefetch=1,
            grid=(cols // wide,),
            in_specs=[pl.BlockSpec((STEP, WIDE), lambda c, t: (0, 0))] * len(vs)
            + [pl.BlockSpec((WIDE, wide), lambda c, t: (0, c))],
            out_specs=[pl.BlockSpec((WIDE, wide), lambda c, t: (0, c))] * 2,
            scratch_shapes=[pltpu.VMEM((WIDE, WIDE), F32)],
        ),
        out_shape=[jax.ShapeDtypeStruct((WIDE, cols), BF16)] * 2,
        compiler_params=pltpu.CompilerParams(vmem_limit_bytes=32 * 2**20),
        cost_estimate=pl.CostEstimate(
            flops=12 * WIDE * WIDE * cols, bytes_accessed=10 * WIDE * cols, transcendentals=0
        ),
        name="right",
    )(tab, *vs, b)


def update_kernel(first, count, nbuf, tab, m_ref, hi_any, lo_any, *refs):
    own, other = refs[:nbuf], refs[nbuf : 2 * nbuf]
    out_ref, lhs, hi_ref, lo_ref, sem, rsem = refs[-6:]
    s = pl.program_id(0)
    cols = m_ref.shape[1]

    def chunk(a, act):
        part = pl.ds(a, NB)
        n = a // NB
        act(pltpu.make_async_copy(hi_any.at[:, part], hi_ref.at[:, part], rsem.at[n, 0]))
        act(pltpu.make_async_copy(lo_any.at[:, part], lo_ref.at[:, part], rsem.at[n, 1]))

    chain, mine, my_row = tab[0], tab[1], tab[2]

    def fetch(n, act):
        slot = lax.rem(n, 2)
        for x in range(nbuf):

            @pl.when(n + chain == x)
            def _(x=x):
                act(pltpu.make_async_copy(own[x], lhs.at[slot, 0], sem.at[slot, 0]))
                act(pltpu.make_async_copy(other[x], lhs.at[slot, 1], sem.at[slot, 1]))

    @pl.when(s == 0)
    def _():
        fetch(s, lambda c: c.start())
        for a in range(0, cols, NB):
            chunk(a, lambda c: c.start())

    @pl.when(s + 1 < count)
    def _():
        fetch(s + 1, lambda c: c.start())

    fetch(s, lambda c: c.wait())
    slot = lax.rem(s, 2)
    oh, ol = split(lhs[slot, 0])
    th, tl = split(lhs[slot, 1])
    left = jnp.concatenate([oh, th, oh, th, ol, tl], 1)
    for a in range(0, cols, NB):

        @pl.when(s == 0)
        def _(a=a):
            chunk(a, lambda c: c.wait())

        rh, rl = hi_ref[:, a : a + NB], lo_ref[:, a : a + NB]
        prod = jnp.dot(
            left, jnp.concatenate([rh, rl, rh], 0), preferred_element_type=F32
        )
        m = m_ref[:, a : a + NB]
        if a == 0:
            m = jnp.where(mine < PANELS, 0.0, m)
        out_ref[:, a : a + NB] = m - prod
    if first == 0:

        @pl.when((s == 0) & (my_row < PANELS))
        def _():
            r = lax.broadcasted_iota(jnp.int32, (NB, NB), 0)
            c = lax.broadcasted_iota(jnp.int32, (NB, NB), 1)
            keep = (mine < PANELS) & ((my_row > mine) | ((my_row == mine) & (r >= c)))
            out_ref[0:NB, 0:NB] = jnp.where(keep, out_ref[0:NB, 0:NB], 0.0)
            if cols > NB:
                out_ref[0:NB, NB:] = jnp.zeros((NB, cols - NB), F32)


def update(tab, first, count, stored, high, low, own, other, prev):
    nrows, cols = stored.shape
    tall = own[0].shape[0]
    args = [stored, high, low, *own, *other] + ([] if prev is None else [prev])
    return pl.pallas_call(
        functools.partial(update_kernel, first, count, len(own)),
        grid_spec=pltpu.PrefetchScalarGridSpec(
            num_scalar_prefetch=1,
            grid=(count,),
            in_specs=[pl.BlockSpec((tall, cols), lambda s, t: (first + s, 0))]
            + [any_spec()] * (len(args) - 1),
            out_specs=pl.BlockSpec((tall, cols), lambda s, t: (first + s, 0)),
            scratch_shapes=[
                pltpu.VMEM((2, PANELS, tall, NB), F32),
                pltpu.VMEM((WIDE, cols), BF16),
                pltpu.VMEM((WIDE, cols), BF16),
                pltpu.SemaphoreType.DMA((2, PANELS)),
                pltpu.SemaphoreType.DMA((cols // NB, 2)),
            ],
        ),
        out_shape=jax.ShapeDtypeStruct((nrows, cols), F32),
        input_output_aliases={} if prev is None else {len(args): 0},
        compiler_params=pltpu.CompilerParams(vmem_limit_bytes=ROOM),
        cost_estimate=pl.CostEstimate(
            flops=6 * count * tall * WIDE * cols,
            bytes_accessed=8 * count * tall * cols + 4 * WIDE * cols,
            transcendentals=0,
        ),
        name="update",
    )(tab, *args)


def after(x, *done):
    return lax.optimization_barrier((x, *done))[0]


def local(mesh, stored):
    rows, cols = mesh.shape["row"], mesh.shape["col"]
    layers, length = rows // PANELS, cols // PANELS
    both = ("row", "col")
    my_row, my_col = lax.axis_index("row"), lax.axis_index("col")
    layer, lane = my_row // PANELS, my_row % PANELS
    link, side = my_col // PANELS, my_col % PANELS
    rtiles = stored.shape[0] // NB
    tall = (2 if rtiles % 2 == 0 else 1) * NB
    pieces = stored.shape[0] // tall
    nsteps = pieces + length - 1
    devices = [
        (y, c, l, f)
        for y in range(layers)
        for c in range(PANELS)
        for l in range(length)
        for f in range(PANELS)
    ]

    def at(y, c, l, f):
        return (y * PANELS + c) * cols + l * PANELS + f

    def move(x, to):
        pairs = [(at(*d), at(*t)) for d in devices if (t := to(*d)) is not None]
        return lax.ppermute(x, both, pairs)

    def pair(flag, x, y, axis):
        return jnp.concatenate([jnp.where(flag, y, x), jnp.where(flag, x, y)], axis)

    corner = stored[0:NB, 0:NB]
    block = corner
    hops = [
        move(corner, lambda y, c, l, f, h=h: (y, c, h, f) if (y, l) == (0, 0) else None)
        for h in range(1, length)
    ]

    def panel(s):
        return stored[s * tall : (s + 1) * tall, 0:NB]

    own, other, along = [], [], None

    def send(s, *done):
        if s == 0:
            cur = panel(0)
        elif s < pieces:
            cur = jnp.where(link == 0, panel(s), along)
        else:
            cur = along
        if done:
            cur = after(cur, *done)
        own.append(cur)
        z = None
        if s < nsteps - 1:
            z = move(
                cur,
                lambda y, c, l, f: (y, c, l + 1, f)
                if 0 <= s - l < pieces and l + 1 < length
                else None,
            )
        other.append(
            move(cur, lambda y, c, l, f: (y, c, l, 1 - f) if 0 <= s - l < pieces else None)
        )
        return z

    along = send(0)
    for h, x in enumerate(hops):
        block = jnp.where(link == h + 1, x, block)
    near, far = block, block
    cross = move(block, lambda y, c, l, f: (y, c, l, 1 - f) if y == 0 else None)
    for h in range(1, layers):
        x = move(block, lambda y, c, l, f: (h, c, l, f) if y == 0 else None)
        y_ = move(block, lambda y, c, l, f: (h, c, l, 1 - f) if y == 0 else None)
        near = jnp.where(layer == h, x, near)
        cross = jnp.where(layer == h, y_, cross)
    line = pair(side == 1, near, cross, 1)
    s_all = pair(lane == 1, line, move(line, lambda y, c, l, f: (y, 1 - c, l, f)), 0)

    along = send(1, block)
    top = after(stored[0:NB, :], near, cross)
    cur, half = top, top
    for h in range(1, layers):
        cur = move(cur, lambda y, c, l, f: (h, c, l, f) if y == h - 1 else None)
        half = jnp.where(layer == h, cur, half)
    mate = move(half, lambda y, c, l, f: (y, 1 - c, l, f))

    flags = jnp.stack([link, my_col, my_row, side]).astype(jnp.int32)
    pair_flags = jnp.stack([my_col, side]).astype(jnp.int32)
    us, vs = [], []
    out, rest = None, 0
    high = low = None
    nblocks = WIDE // STEP
    dep = [s_all]
    for s in range(2, nsteps + 1):
        if s < nsteps:
            along = send(s, *dep, other[s - 2])
        dep = []
        if len(us) < nblocks:
            u, v = factor(s_all, us, vs)
            us.append(u)
            vs.append(v)
            dep = [v]
        elif high is None:
            high, low = right(pair_flags, vs, pair(lane == 1, half, mate, 0))
            dep = [low]
        else:
            stop = min(rest + 2, s - length + 1, pieces)
            if stop > rest:
                out = run_update(flags, rest, stop, stored, high, low, own, other, out, length)
                rest = stop
                dep = [out]
    while len(us) < nblocks:
        u, v = factor(s_all, us, vs)
        us.append(u)
        vs.append(v)
    if high is None:
        high, low = right(pair_flags, vs, pair(lane == 1, half, mate, 0))
    cuts = [pieces] if pieces > rest else []
    for stop in cuts:
        out = run_update(flags, rest, stop, stored, high, low, own, other, out, length)
        rest = stop
    return out


def run_update(flags, first, stop, stored, high, low, own, other, prev, length):
    lo, hi = first, stop + length - 1
    return update(
        flags, first, stop - first, stored, high, low, own[lo:hi], other[lo:hi], prev
    )


def solution(mesh):
    return jax.shard_map(
        functools.partial(local, mesh),
        mesh=mesh,
        in_specs=(P("row", "col"),),
        out_specs=P("row", "col"),
        check_vma=False,
    )
```

```python
import functools

import jax
import jax.numpy as jnp
from jax import lax
from jax.experimental import pallas as pl
from jax.experimental.pallas import tpu as pltpu
from jax.sharding import PartitionSpec as P

NB = 256
PANELS = 2
WIDE = PANELS * NB
STEP = 128
SUB = 16
LAG = 2
ROOM = 58 * 2**20
HIGHEST = lax.Precision.HIGHEST
F32 = jnp.float32
BF16 = jnp.bfloat16


def any_spec():
    return pl.BlockSpec(memory_space=pl.ANY)


def dot(a, b, dims):
    return lax.dot_general(
        a, b, ((dims[0], dims[1]), ((), ())), precision=HIGHEST, preferred_element_type=F32
    )


def eliminate(work, start):
    rows = work[start : start + SUB, :]
    lanes = rows.shape[1]
    shape = (SUB, STEP)
    sub = lax.broadcasted_iota(jnp.int32, shape, 0)
    cols = [jnp.broadcast_to(rows[:, start + c : start + c + 1], shape) for c in range(SUB)]
    parts = [rows[:, a : a + STEP] for a in range(0, lanes, STEP)]
    scale = jnp.ones(shape, F32)

    def line(x, c):
        return jnp.broadcast_to(x[c : c + 1, :], shape)

    def inverse(x):
        r = pl.reciprocal(x, approx=True)
        r = r * (2.0 - x * r)
        return r * (2.0 - x * r)

    for c in range(0, SUB, 2):
        p, q = cols[c], cols[c + 1]
        a, b, d = line(p, c), line(q, c), line(q, c + 1)
        det = a * d - b * b
        r, ra = inverse(det), inverse(a)
        f = jnp.where(sub > c + 1, (p * d - q * b) * r, jnp.where(sub == c + 1, b * ra, 0.0))
        g = jnp.where(sub > c + 1, (q * a - p * b) * r, 0.0)
        scale = jnp.where(sub == c, a, jnp.where(sub == c + 1, det * ra, scale))
        for e in range(c + 2, SUB):
            cols[e] = cols[e] - f * line(cols[e], c) - g * line(cols[e], c + 1)
        parts = [x - f * line(x, c) - g * line(x, c + 1) for x in parts]
    root = lax.rsqrt(scale)
    root = root * (1.5 - 0.5 * scale * root * root)
    return jnp.concatenate([x * root for x in parts], 1)


def factor_kernel(block, s_ref, *refs):
    us, vs = refs[:block], refs[block : 2 * block]
    u_ref, v_ref, work = refs[2 * block :]
    lo, hi = block * STEP, (block + 1) * STEP
    eye = (
        lax.broadcasted_iota(jnp.int32, (STEP, STEP), 0)
        == lax.broadcasted_iota(jnp.int32, (STEP, STEP), 1)
    ).astype(F32)
    row = s_ref[:, lo:]
    if lo:
        left = jnp.concatenate([x[:, lo:hi] for x in us], 0)
        row = row - dot(left, jnp.concatenate([x[:, lo:] for x in us], 0), ((0,), (0,)))
        inv = -dot(left, jnp.concatenate([x[:, 0:lo] for x in vs], 0), ((0,), (0,)))
        u_ref[:, 0:lo] = jnp.zeros((STEP, lo), F32)
    work[:, 0:STEP] = row[:, 0:STEP]
    work[:, STEP:] = eye
    lanes = lax.broadcasted_iota(jnp.int32, (SUB, 2 * STEP), 1)
    for start in range(0, STEP, SUB):
        done = eliminate(work, start)
        work[start : start + SUB, :] = jnp.where(lanes >= start, done, 0.0)
        if start + SUB < STEP:
            rest = work[start + SUB :, :]
            work[start + SUB :, :] = rest - dot(
                done[:, start + SUB : STEP], done, ((0,), (0,))
            )
    dinv = work[:, STEP:]
    u_ref[:, lo:hi] = work[:, 0:STEP]
    v_ref[:, lo:hi] = dinv
    if hi < WIDE:
        u_ref[:, hi:] = dot(dinv, row[:, STEP:], ((1,), (0,)))
        v_ref[:, hi:] = jnp.zeros((STEP, WIDE - hi), F32)
    if lo:
        v_ref[:, 0:lo] = dot(dinv, inv, ((1,), (0,)))


def factor(s, us, vs):
    block = len(us)
    line = pl.BlockSpec((STEP, WIDE), lambda i: (0, 0))
    return pl.pallas_call(
        functools.partial(factor_kernel, block),
        grid=(1,),
        in_specs=[pl.BlockSpec((STEP, WIDE), lambda i: (block, 0))] + [line] * (2 * block),
        out_specs=[line] * 2,
        out_shape=[jax.ShapeDtypeStruct((STEP, WIDE), F32)] * 2,
        scratch_shapes=[pltpu.VMEM((STEP, 2 * STEP), F32)],
        compiler_params=pltpu.CompilerParams(vmem_limit_bytes=24 * 2**20),
        cost_estimate=pl.CostEstimate(
            flops=6 * 10**9, bytes_accessed=6 * 2**20, transcendentals=0
        ),
        name="factor",
    )(s, *us, *vs)


def split(x):
    high = x.astype(BF16)
    return high, (x - high.astype(F32)).astype(BF16)


def right_kernel(blocks, tab, *refs):
    vs = refs[:blocks]
    b_ref, hi_ref, lo_ref, sinv = refs[blocks:]
    mine, side = tab[0], tab[1]

    @pl.when(pl.program_id(0) == 0)
    def _():
        v = jnp.concatenate([x[...] for x in vs], 0)
        sinv[...] = dot(v, v, ((0,), (0,)))

    def place(k):
        return pl.ds(pl.multiple_of(lax.rem(k + PANELS - side, PANELS) * NB, NB), NB)

    for k in range(PANELS):
        high, low = split(dot(sinv[k * NB : (k + 1) * NB, :], b_ref[...], ((1,), (0,))))
        hi_ref[place(k), :] = high
        lo_ref[place(k), :] = low
    for j in range(PANELS):

        @pl.when((pl.program_id(0) == 0) & (mine == j))
        def _(j=j):
            for k in range(PANELS):
                for m in range(NB // STEP):
                    part = vs[j * (NB // STEP) + m][:, k * NB : (k + 1) * NB]
                    high, low = split(-part.T)
                    hi_ref[place(k), m * STEP : (m + 1) * STEP] = high
                    lo_ref[place(k), m * STEP : (m + 1) * STEP] = low


def right(tab, vs, b):
    cols = b.shape[1]
    wide = min(cols, 512)
    return pl.pallas_call(
        functools.partial(right_kernel, len(vs)),
        grid_spec=pltpu.PrefetchScalarGridSpec(
            num_scalar_prefetch=1,
            grid=(cols // wide,),
            in_specs=[pl.BlockSpec((STEP, WIDE), lambda c, t: (0, 0))] * len(vs)
            + [pl.BlockSpec((WIDE, wide), lambda c, t: (0, c))],
            out_specs=[pl.BlockSpec((WIDE, wide), lambda c, t: (0, c))] * 2,
            scratch_shapes=[pltpu.VMEM((WIDE, WIDE), F32)],
        ),
        out_shape=[jax.ShapeDtypeStruct((WIDE, cols), BF16)] * 2,
        compiler_params=pltpu.CompilerParams(vmem_limit_bytes=32 * 2**20),
        cost_estimate=pl.CostEstimate(
            flops=12 * WIDE * WIDE * cols, bytes_accessed=10 * WIDE * cols, transcendentals=0
        ),
        name="right",
    )(tab, *vs, b)


def update_kernel(first, count, nbuf, tab, m_ref, hi_ref, lo_ref, *refs):
    own, other = refs[:nbuf], refs[nbuf : 2 * nbuf]
    out_ref, lhs, sem = refs[-3:]
    s = pl.program_id(0)
    cols = m_ref.shape[1]
    chain, mine, my_row = tab[0], tab[1], tab[2]

    def fetch(n, act):
        slot = lax.rem(n, 2)
        for x in range(nbuf):

            @pl.when(n + LAG * chain == x)
            def _(x=x):
                act(pltpu.make_async_copy(own[x], lhs.at[slot, 0], sem.at[slot, 0]))
                act(pltpu.make_async_copy(other[x], lhs.at[slot, 1], sem.at[slot, 1]))

    @pl.when(s == 0)
    def _():
        fetch(s, lambda c: c.start())

    @pl.when(s + 1 < count)
    def _():
        fetch(s + 1, lambda c: c.start())

    fetch(s, lambda c: c.wait())
    slot = lax.rem(s, 2)
    oh, ol = split(lhs[slot, 0])
    th, tl = split(lhs[slot, 1])
    left = jnp.concatenate([oh, th, oh, th, ol, tl], 1)
    for a in range(0, cols, NB):
        rh, rl = hi_ref[:, a : a + NB], lo_ref[:, a : a + NB]
        prod = jnp.dot(
            left, jnp.concatenate([rh, rl, rh], 0), preferred_element_type=F32
        )
        m = m_ref[:, a : a + NB]
        if a == 0:
            m = jnp.where(mine < PANELS, 0.0, m)
        out_ref[:, a : a + NB] = m - prod
    if first == 0:

        @pl.when((s == 0) & (my_row < PANELS))
        def _():
            r = lax.broadcasted_iota(jnp.int32, (NB, NB), 0)
            c = lax.broadcasted_iota(jnp.int32, (NB, NB), 1)
            keep = (mine < PANELS) & ((my_row > mine) | ((my_row == mine) & (r >= c)))
            out_ref[0:NB, 0:NB] = jnp.where(keep, out_ref[0:NB, 0:NB], 0.0)
            if cols > NB:
                out_ref[0:NB, NB:] = jnp.zeros((NB, cols - NB), F32)


def update(tab, first, count, stored, high, low, own, other, prev):
    nrows, cols = stored.shape
    tall = own[0].shape[0]
    args = [stored, high, low, *own, *other] + ([] if prev is None else [prev])
    return pl.pallas_call(
        functools.partial(update_kernel, first, count, len(own)),
        grid_spec=pltpu.PrefetchScalarGridSpec(
            num_scalar_prefetch=1,
            grid=(count,),
            in_specs=[pl.BlockSpec((tall, cols), lambda s, t: (first + s, 0))]
            + [pl.BlockSpec(memory_space=pltpu.VMEM)] * 2
            + [any_spec()] * (len(args) - 3),
            out_specs=pl.BlockSpec((tall, cols), lambda s, t: (first + s, 0)),
            scratch_shapes=[
                pltpu.VMEM((2, PANELS, tall, NB), F32),
                pltpu.SemaphoreType.DMA((2, PANELS)),
            ],
        ),
        out_shape=jax.ShapeDtypeStruct((nrows, cols), F32),
        input_output_aliases={} if prev is None else {len(args): 0},
        compiler_params=pltpu.CompilerParams(vmem_limit_bytes=ROOM),
        cost_estimate=pl.CostEstimate(
            flops=6 * count * tall * WIDE * cols,
            bytes_accessed=8 * count * tall * cols + 4 * WIDE * cols,
            transcendentals=0,
        ),
        name="update",
    )(tab, *args)


def pick_kernel(start, tab, stored, along, *refs):
    out, sem = refs[-2:]

    @pl.when(tab[0] == 0)
    def _():
        tall, wide = out.shape
        copy = pltpu.make_async_copy(
            stored.at[pl.ds(start, tall), pl.ds(0, wide)], out, sem.at[0]
        )
        copy.start()
        copy.wait()

    @pl.when(tab[0] != 0)
    def _():
        out[...] = along[...]


def pick(tab, start, stored, along, done):
    vmem = pl.BlockSpec(memory_space=pltpu.VMEM)
    return pl.pallas_call(
        functools.partial(pick_kernel, start),
        grid_spec=pltpu.PrefetchScalarGridSpec(
            num_scalar_prefetch=1,
            grid=(),
            in_specs=[any_spec(), vmem] + [any_spec()] * len(done),
            out_specs=vmem,
            scratch_shapes=[pltpu.SemaphoreType.DMA((1,))],
        ),
        out_shape=jax.ShapeDtypeStruct(along.shape, F32),
        compiler_params=pltpu.CompilerParams(vmem_limit_bytes=40 * 2**20),
        cost_estimate=pl.CostEstimate(
            flops=0, bytes_accessed=8 * along.shape[0] * NB, transcendentals=0
        ),
        name="pick",
    )(tab, stored, along, *done)


def after(x, *done):
    return lax.optimization_barrier((x, *done))[0]


def local(mesh, stored):
    rows, cols = mesh.shape["row"], mesh.shape["col"]
    layers, length = rows // PANELS, cols // PANELS
    both = ("row", "col")
    my_row, my_col = lax.axis_index("row"), lax.axis_index("col")
    layer, lane = my_row // PANELS, my_row % PANELS
    link, side = my_col // PANELS, my_col % PANELS
    rtiles = stored.shape[0] // NB
    tall = (2 if rtiles % 2 == 0 else 1) * NB
    pieces = stored.shape[0] // tall
    nsteps = pieces + LAG * (length - 1)
    devices = [
        (y, c, l, f)
        for y in range(layers)
        for c in range(PANELS)
        for l in range(length)
        for f in range(PANELS)
    ]

    def at(y, c, l, f):
        return (y * PANELS + c) * cols + l * PANELS + f

    def move(x, to):
        pairs = [(at(*d), at(*t)) for d in devices if (t := to(*d)) is not None]
        return lax.ppermute(x, both, pairs)

    def pair(flag, x, y, axis):
        return jnp.concatenate([jnp.where(flag, y, x), jnp.where(flag, x, y)], axis)

    corner = stored[0:NB, 0:NB]
    block = corner
    hops = [
        move(corner, lambda y, c, l, f, h=h: (y, c, h, f) if (y, l) == (0, 0) else None)
        for h in range(1, length)
    ]

    def panel(s):
        return stored[s * tall : (s + 1) * tall, 0:NB]

    own, other, along = [], [], []
    chain = link.astype(jnp.int32)[None]

    def live(s, l):
        return 0 <= s - LAG * l < pieces

    def send(s, *done):
        if s < min(LAG, pieces):
            cur = panel(s)
        elif s < pieces:
            cur = pick(chain, s * tall, stored, along[s - LAG], done)
            done = ()
        else:
            cur = along[s - LAG]
        if done:
            cur = after(cur, *done)
        own.append(cur)
        along.append(
            move(
                cur,
                lambda y, c, l, f: (y, c, l + 1, f) if live(s, l) and l + 1 < length else None,
            )
            if any(live(s, l) for l in range(length - 1))
            else cur
        )
        other.append(move(cur, lambda y, c, l, f: (y, c, l, 1 - f) if live(s, l) else None))

    send(0)
    for h, x in enumerate(hops):
        block = jnp.where(link == h + 1, x, block)
    near, far = block, block
    cross = move(block, lambda y, c, l, f: (y, c, l, 1 - f) if y == 0 else None)
    for h in range(1, layers):
        x = move(block, lambda y, c, l, f: (h, c, l, f) if y == 0 else None)
        y_ = move(block, lambda y, c, l, f: (h, c, l, 1 - f) if y == 0 else None)
        near = jnp.where(layer == h, x, near)
        cross = jnp.where(layer == h, y_, cross)
    line = pair(side == 1, near, cross, 1)
    s_all = pair(lane == 1, line, move(line, lambda y, c, l, f: (y, 1 - c, l, f)), 0)

    send(1)
    top = after(stored[0:NB, :], near, cross)
    cur, half = top, top
    for h in range(1, layers):
        cur = move(cur, lambda y, c, l, f: (h, c, l, f) if y == h - 1 else None)
        half = jnp.where(layer == h, cur, half)
    mate = move(half, lambda y, c, l, f: (y, 1 - c, l, f))

    flags = jnp.stack([link, my_col, my_row, side]).astype(jnp.int32)
    pair_flags = jnp.stack([my_col, side]).astype(jnp.int32)
    us, vs = [], []
    out, rest = None, 0
    high = low = None
    nblocks = WIDE // STEP
    dep = []
    for s in range(2, nsteps + 1):
        if s < nsteps:
            send(s, *dep, other[s - LAG], own[s - 1])
        dep = []
        if len(us) < nblocks:
            if s > LAG:
                for _ in range(2):
                    u, v = factor(s_all, us, vs)
                    us.append(u)
                    vs.append(v)
                dep = [v]
        elif high is None and s >= nsteps // 2 - 1:
            high, low = right(pair_flags, vs, pair(lane == 1, half, mate, 0))
            dep = [low]
        elif high is not None:
            stop = min(rest + 2, s - LAG * length + 1, pieces)
            if stop == rest + 2:
                out = run_update(flags, rest, stop, stored, high, low, own, other, out, length)
                rest = stop
                dep = [out]
    while len(us) < nblocks:
        u, v = factor(s_all, us, vs)
        us.append(u)
        vs.append(v)
    if high is None:
        high, low = right(pair_flags, vs, pair(lane == 1, half, mate, 0))
    cuts = [pieces] if pieces > rest else []
    for stop in cuts:
        out = run_update(flags, rest, stop, stored, high, low, own, other, out, length)
        rest = stop
    return out


def run_update(flags, first, stop, stored, high, low, own, other, prev, length):
    lo, hi = first, stop + LAG * (length - 1)
    return update(
        flags, first, stop - first, stored, high, low, own[lo:hi], other[lo:hi], prev
    )


def solution(mesh):
    return jax.shard_map(
        functools.partial(local, mesh),
        mesh=mesh,
        in_specs=(P("row", "col"),),
        out_specs=P("row", "col"),
        check_vma=False,
    )
```

```python
import functools

import jax
import jax.numpy as jnp
from jax import lax
from jax.experimental import pallas as pl
from jax.experimental.pallas import tpu as pltpu
from jax.sharding import PartitionSpec as P

NB = 256
PANELS = 2
WIDE = PANELS * NB
STEP = 128
SUB = 16
LAG = 2
ROOM = 58 * 2**20
HIGHEST = lax.Precision.HIGHEST
F32 = jnp.float32
BF16 = jnp.bfloat16


def any_spec():
    return pl.BlockSpec(memory_space=pl.ANY)


def dot(a, b, dims):
    return lax.dot_general(
        a, b, ((dims[0], dims[1]), ((), ())), precision=HIGHEST, preferred_element_type=F32
    )


def eliminate(work, start):
    rows = work[start : start + SUB, :]
    lanes = rows.shape[1]
    shape = (SUB, STEP)
    sub = lax.broadcasted_iota(jnp.int32, shape, 0)
    cols = [jnp.broadcast_to(rows[:, start + c : start + c + 1], shape) for c in range(SUB)]
    parts = [rows[:, a : a + STEP] for a in range(0, lanes, STEP)]
    scale = jnp.ones(shape, F32)

    def line(x, c):
        return jnp.broadcast_to(x[c : c + 1, :], shape)

    def inverse(x):
        r = pl.reciprocal(x, approx=True)
        r = r * (2.0 - x * r)
        return r * (2.0 - x * r)

    for c in range(0, SUB, 2):
        p, q = cols[c], cols[c + 1]
        a, b, d = line(p, c), line(q, c), line(q, c + 1)
        det = a * d - b * b
        r, ra = inverse(det), inverse(a)
        f = jnp.where(sub > c + 1, (p * d - q * b) * r, jnp.where(sub == c + 1, b * ra, 0.0))
        g = jnp.where(sub > c + 1, (q * a - p * b) * r, 0.0)
        scale = jnp.where(sub == c, a, jnp.where(sub == c + 1, det * ra, scale))
        for e in range(c + 2, SUB):
            cols[e] = cols[e] - f * line(cols[e], c) - g * line(cols[e], c + 1)
        parts = [x - f * line(x, c) - g * line(x, c + 1) for x in parts]
    root = lax.rsqrt(scale)
    root = root * (1.5 - 0.5 * scale * root * root)
    return jnp.concatenate([x * root for x in parts], 1)


def factor_kernel(block, s_ref, *refs):
    us, vs = refs[:block], refs[block : 2 * block]
    u_ref, v_ref, work = refs[2 * block :]
    lo, hi = block * STEP, (block + 1) * STEP
    eye = (
        lax.broadcasted_iota(jnp.int32, (STEP, STEP), 0)
        == lax.broadcasted_iota(jnp.int32, (STEP, STEP), 1)
    ).astype(F32)
    row = s_ref[:, lo:]
    if lo:
        left = jnp.concatenate([x[:, lo:hi] for x in us], 0)
        row = row - dot(left, jnp.concatenate([x[:, lo:] for x in us], 0), ((0,), (0,)))
        inv = -dot(left, jnp.concatenate([x[:, 0:lo] for x in vs], 0), ((0,), (0,)))
        u_ref[:, 0:lo] = jnp.zeros((STEP, lo), F32)
    work[:, 0:STEP] = row[:, 0:STEP]
    work[:, STEP:] = eye
    lanes = lax.broadcasted_iota(jnp.int32, (SUB, 2 * STEP), 1)
    for start in range(0, STEP, SUB):
        done = eliminate(work, start)
        work[start : start + SUB, :] = jnp.where(lanes >= start, done, 0.0)
        if start + SUB < STEP:
            rest = work[start + SUB :, :]
            work[start + SUB :, :] = rest - dot(
                done[:, start + SUB : STEP], done, ((0,), (0,))
            )
    dinv = work[:, STEP:]
    u_ref[:, lo:hi] = work[:, 0:STEP]
    v_ref[:, lo:hi] = dinv
    if hi < WIDE:
        u_ref[:, hi:] = dot(dinv, row[:, STEP:], ((1,), (0,)))
        v_ref[:, hi:] = jnp.zeros((STEP, WIDE - hi), F32)
    if lo:
        v_ref[:, 0:lo] = dot(dinv, inv, ((1,), (0,)))


def factor(s, us, vs):
    block = len(us)
    line = pl.BlockSpec((STEP, WIDE), lambda i: (0, 0))
    return pl.pallas_call(
        functools.partial(factor_kernel, block),
        grid=(1,),
        in_specs=[pl.BlockSpec((STEP, WIDE), lambda i: (block, 0))] + [line] * (2 * block),
        out_specs=[line] * 2,
        out_shape=[jax.ShapeDtypeStruct((STEP, WIDE), F32)] * 2,
        scratch_shapes=[pltpu.VMEM((STEP, 2 * STEP), F32)],
        compiler_params=pltpu.CompilerParams(vmem_limit_bytes=24 * 2**20),
        cost_estimate=pl.CostEstimate(flops=0, bytes_accessed=4096, transcendentals=0),
        name="factor",
    )(s, *us, *vs)


def split(x):
    high = x.astype(BF16)
    return high, (x - high.astype(F32)).astype(BF16)


def right_kernel(blocks, tab, *refs):
    vs = refs[:blocks]
    b_ref, hi_ref, lo_ref, sinv = refs[blocks:]
    mine, side = tab[0], tab[1]

    @pl.when(pl.program_id(0) == 0)
    def _():
        v = jnp.concatenate([x[...] for x in vs], 0)
        sinv[...] = dot(v, v, ((0,), (0,)))

    def place(k):
        return pl.ds(pl.multiple_of(lax.rem(k + PANELS - side, PANELS) * NB, NB), NB)

    for k in range(PANELS):
        high, low = split(dot(sinv[k * NB : (k + 1) * NB, :], b_ref[...], ((1,), (0,))))
        hi_ref[place(k), :] = high
        lo_ref[place(k), :] = low
    for j in range(PANELS):

        @pl.when((pl.program_id(0) == 0) & (mine == j))
        def _(j=j):
            for k in range(PANELS):
                for m in range(NB // STEP):
                    part = vs[j * (NB // STEP) + m][:, k * NB : (k + 1) * NB]
                    high, low = split(-part.T)
                    hi_ref[place(k), m * STEP : (m + 1) * STEP] = high
                    lo_ref[place(k), m * STEP : (m + 1) * STEP] = low


def right(tab, vs, b):
    cols = b.shape[1]
    wide = min(cols, 512)
    return pl.pallas_call(
        functools.partial(right_kernel, len(vs)),
        grid_spec=pltpu.PrefetchScalarGridSpec(
            num_scalar_prefetch=1,
            grid=(cols // wide,),
            in_specs=[pl.BlockSpec((STEP, WIDE), lambda c, t: (0, 0))] * len(vs)
            + [pl.BlockSpec((WIDE, wide), lambda c, t: (0, c))],
            out_specs=[pl.BlockSpec((WIDE, wide), lambda c, t: (0, c))] * 2,
            scratch_shapes=[pltpu.VMEM((WIDE, WIDE), F32)],
        ),
        out_shape=[jax.ShapeDtypeStruct((WIDE, cols), BF16)] * 2,
        compiler_params=pltpu.CompilerParams(vmem_limit_bytes=32 * 2**20),
        cost_estimate=pl.CostEstimate(flops=0, bytes_accessed=4096, transcendentals=0),
        name="right",
    )(tab, *vs, b)


def update_kernel(first, count, nbuf, tab, m_ref, hi_ref, lo_ref, *refs):
    own, other = refs[:nbuf], refs[nbuf : 2 * nbuf]
    out_ref, lhs, sem = refs[-3:]
    s = pl.program_id(0)
    cols = m_ref.shape[1]
    chain, mine, my_row = tab[0], tab[1], tab[2]

    parts = own[0].shape[0] // NB

    def fetch(n, act):
        slot = lax.rem(n, 2)
        part = pl.ds(pl.multiple_of(lax.rem(n, parts) * NB, NB), NB)
        for x in range(nbuf):

            @pl.when(n // parts + LAG * chain == x)
            def _(x=x):
                act(pltpu.make_async_copy(own[x].at[part, :], lhs.at[slot, 0], sem.at[slot, 0]))
                act(
                    pltpu.make_async_copy(other[x].at[part, :], lhs.at[slot, 1], sem.at[slot, 1])
                )

    @pl.when(s == 0)
    def _():
        fetch(s, lambda c: c.start())

    @pl.when(s + 1 < count * parts)
    def _():
        fetch(s + 1, lambda c: c.start())

    fetch(s, lambda c: c.wait())
    slot = lax.rem(s, 2)
    oh, ol = split(lhs[slot, 0])
    th, tl = split(lhs[slot, 1])
    left = jnp.concatenate([oh, th, oh, th, ol, tl], 1)
    for a in range(0, cols, NB):
        rh, rl = hi_ref[:, a : a + NB], lo_ref[:, a : a + NB]
        prod = jnp.dot(
            left, jnp.concatenate([rh, rl, rh], 0), preferred_element_type=F32
        )
        m = m_ref[:, a : a + NB]
        if a == 0:
            m = jnp.where(mine < PANELS, 0.0, m)
        out_ref[:, a : a + NB] = m - prod
    if first == 0:

        @pl.when((s == 0) & (my_row < PANELS))
        def _():
            r = lax.broadcasted_iota(jnp.int32, (NB, NB), 0)
            c = lax.broadcasted_iota(jnp.int32, (NB, NB), 1)
            keep = (mine < PANELS) & ((my_row > mine) | ((my_row == mine) & (r >= c)))
            out_ref[:, 0:NB] = jnp.where(keep, out_ref[:, 0:NB], 0.0)
            if cols > NB:
                out_ref[:, NB:] = jnp.zeros((NB, cols - NB), F32)


def update(tab, first, count, stored, high, low, own, other, prev):
    nrows, cols = stored.shape
    tall = own[0].shape[0]
    parts = tall // NB
    args = [stored, high, low, *own, *other] + ([] if prev is None else [prev])
    return pl.pallas_call(
        functools.partial(update_kernel, first, count, len(own)),
        grid_spec=pltpu.PrefetchScalarGridSpec(
            num_scalar_prefetch=1,
            grid=(count * parts,),
            in_specs=[pl.BlockSpec((NB, cols), lambda s, t: (first * parts + s, 0))]
            + [pl.BlockSpec(memory_space=pltpu.VMEM)] * 2
            + [any_spec()] * (len(args) - 3),
            out_specs=pl.BlockSpec((NB, cols), lambda s, t: (first * parts + s, 0)),
            scratch_shapes=[
                pltpu.VMEM((2, PANELS, NB, NB), F32),
                pltpu.SemaphoreType.DMA((2, PANELS)),
            ],
        ),
        out_shape=jax.ShapeDtypeStruct((nrows, cols), F32),
        input_output_aliases={} if prev is None else {len(args): 0},
        compiler_params=pltpu.CompilerParams(vmem_limit_bytes=ROOM),
        cost_estimate=pl.CostEstimate(flops=0, bytes_accessed=4096, transcendentals=0),
        name="update",
    )(tab, *args)


def pick_kernel(start, tab, stored, along, *refs):
    out, sem = refs[-2:]

    @pl.when(tab[0] == 0)
    def _():
        tall, wide = out.shape
        copy = pltpu.make_async_copy(
            stored.at[pl.ds(start, tall), pl.ds(0, wide)], out, sem.at[0]
        )
        copy.start()
        copy.wait()

    @pl.when(tab[0] != 0)
    def _():
        out[...] = along[...]


def pick(tab, start, stored, along, done):
    vmem = pl.BlockSpec(memory_space=pltpu.VMEM)
    return pl.pallas_call(
        functools.partial(pick_kernel, start),
        grid_spec=pltpu.PrefetchScalarGridSpec(
            num_scalar_prefetch=1,
            grid=(),
            in_specs=[any_spec(), vmem] + [any_spec()] * len(done),
            out_specs=vmem,
            scratch_shapes=[pltpu.SemaphoreType.DMA((1,))],
        ),
        out_shape=jax.ShapeDtypeStruct(along.shape, F32),
        compiler_params=pltpu.CompilerParams(vmem_limit_bytes=40 * 2**20),
        cost_estimate=pl.CostEstimate(flops=0, bytes_accessed=4096, transcendentals=0),
        name="pick",
    )(tab, stored, along, *done)


def after(x, *done):
    return lax.optimization_barrier((x, *done))[0]


def local(mesh, stored):
    rows, cols = mesh.shape["row"], mesh.shape["col"]
    layers, length = rows // PANELS, cols // PANELS
    both = ("row", "col")
    my_row, my_col = lax.axis_index("row"), lax.axis_index("col")
    layer, lane = my_row // PANELS, my_row % PANELS
    link, side = my_col // PANELS, my_col % PANELS
    rtiles = stored.shape[0] // NB
    tall = (2 if rtiles % 2 == 0 else 1) * NB
    pieces = stored.shape[0] // tall
    nsteps = pieces + LAG * (length - 1)
    devices = [
        (y, c, l, f)
        for y in range(layers)
        for c in range(PANELS)
        for l in range(length)
        for f in range(PANELS)
    ]

    def at(y, c, l, f):
        return (y * PANELS + c) * cols + l * PANELS + f

    def move(x, to):
        pairs = [(at(*d), at(*t)) for d in devices if (t := to(*d)) is not None]
        return lax.ppermute(x, both, pairs)

    def pair(flag, x, y, axis):
        return jnp.concatenate([jnp.where(flag, y, x), jnp.where(flag, x, y)], axis)

    corner = stored[0:NB, 0:NB]
    block = corner
    hops = [
        move(corner, lambda y, c, l, f, h=h: (y, c, h, f) if (y, l) == (0, 0) else None)
        for h in range(1, length)
    ]

    def panel(s):
        return stored[s * tall : (s + 1) * tall, 0:NB]

    own, other, along = [], [], []
    chain = link.astype(jnp.int32)[None]

    def live(s, l):
        return 0 <= s - LAG * l < pieces

    def send(s, *done):
        if s < min(LAG, pieces):
            cur = panel(s)
        elif s < pieces:
            cur = pick(chain, s * tall, stored, along[s - LAG], done)
            done = ()
        else:
            cur = along[s - LAG]
        if done:
            cur = after(cur, *done)
        own.append(cur)
        along.append(
            move(
                cur,
                lambda y, c, l, f: (y, c, l + 1, f) if live(s, l) and l + 1 < length else None,
            )
            if any(live(s, l) for l in range(length - 1))
            else cur
        )
        other.append(move(cur, lambda y, c, l, f: (y, c, l, 1 - f) if live(s, l) else None))

    send(0)
    for h, x in enumerate(hops):
        block = jnp.where(link == h + 1, x, block)
    block = after(block, along[0], other[0])
    send(1)
    near = block
    cross = move(block, lambda y, c, l, f: (y, c, l, 1 - f) if y == 0 else None)
    for h in range(1, layers):
        x = move(block, lambda y, c, l, f: (h, c, l, f) if y == 0 else None)
        y_ = move(block, lambda y, c, l, f: (h, c, l, 1 - f) if y == 0 else None)
        near = jnp.where(layer == h, x, near)
        cross = jnp.where(layer == h, y_, cross)
    mine, facing = lax.optimization_barrier((near, cross, along[1], other[1]))[:2]
    line = pair(side == 1, mine, facing, 1)
    s_all = pair(lane == 1, line, move(line, lambda y, c, l, f: (y, 1 - c, l, f)), 0)

    top = after(stored[0:NB, :], near, cross)
    cur, half = top, top
    for h in range(1, layers):
        cur = move(cur, lambda y, c, l, f: (h, c, l, f) if y == h - 1 else None)
        half = jnp.where(layer == h, cur, half)

    flags = jnp.stack([link, my_col, my_row, side]).astype(jnp.int32)
    pair_flags = jnp.stack([my_col, side]).astype(jnp.int32)
    us, vs = [], []

    def leading(half, vs):
        half = after(half, vs[-1])
        mate = move(half, lambda y, c, l, f: (y, 1 - c, l, f))
        return pair(lane == 1, half, mate, 0)

    out, rest = None, 0
    high = low = None
    nblocks = WIDE // STEP
    dep = []
    for s in range(2, nsteps + 1):
        if s < nsteps:
            send(s, *dep, other[s - LAG], own[s - 1])
        dep = []
        if len(us) < nblocks:
            if s > LAG and (s - LAG) % 2:
                s_all = after(s_all, own[min(s, nsteps - 1)])
                for _ in range(2):
                    u, v = factor(s_all, us, vs)
                    us.append(u)
                    vs.append(v)
                dep = [v]
        elif high is None and s >= nsteps // 2 - 1:
            b = leading(after(half, own[min(s, nsteps) - 1]), vs)
            high, low = right(pair_flags, vs, b)
            dep = [low]
        elif high is not None:
            stop = min(rest + 3, s - LAG * length + 1, pieces)
            if stop == rest + 3:
                high = after(high, own[min(s, nsteps - 1)])
                out = run_update(flags, rest, stop, stored, high, low, own, other, out, length)
                rest = stop
                dep = [out]
    while len(us) < nblocks:
        u, v = factor(s_all, us, vs)
        us.append(u)
        vs.append(v)
    if high is None:
        high, low = right(pair_flags, vs, leading(half, vs))
    cuts = [pieces] if pieces > rest else []
    for stop in cuts:
        out = run_update(flags, rest, stop, stored, high, low, own, other, out, length)
        rest = stop
    return out


def run_update(flags, first, stop, stored, high, low, own, other, prev, length):
    lo, hi = first, stop + LAG * (length - 1)
    return update(
        flags, first, stop - first, stored, high, low, own[lo:hi], other[lo:hi], prev
    )


def solution(mesh):
    return jax.shard_map(
        functools.partial(local, mesh),
        mesh=mesh,
        in_specs=(P("row", "col"),),
        out_specs=P("row", "col"),
        check_vma=False,
    )
```
